32 devices in a mesh: seq: 8 (over z, x), dp: 4 (over y, core).
Axes of the slice: x: 2, y: 2, z: 4, core: 2. Of those that a mesh axis runs over, the one named last changes fastest.
Arguments:
- signal: bfloat16 [16384, 128], P(('seq', 'dp')), may hold values from -6 to 6
- filter_param: bfloat16 [16384, 128], P(('seq', 'dp')), may hold values from -6 to 6
- skip_gain: float32 [128], replicated, may hold values from 0.5 to 1.5
- out_grad: bfloat16 [16384, 128], P(('seq', 'dp')), may hold values from -6 to 6
Outputs:
- conv_out: bfloat16 [16384, 128], P(('seq', 'dp'))
- input_grad: bfloat16 [16384, 128], P(('seq', 'dp'))
- filter_grad: float32 [16384, 128], P(('seq', 'dp'))
The draws below stay inside these ranges and needn't reach their ends.
All inputs are finite; a program needn't handle non-finite values.
Results may differ from the reference program's by a relative error of at most 0.001.
Values may be sent and summed in bfloat16 or wider, within the bound.
A program may use at most 64 MiB of HBM per device.

```python
import math
import jax
import jax.numpy as jnp

CHANNELS = 128
LENGTH = 16384


def shard_levels(key, shape, shards, low, high):
    def one(axis_at, blocks):
        heights = jax.random.uniform(jax.random.fold_in(jax.random.fold_in(key, 6), axis_at), (blocks,), jnp.float32, low / len(shards), high / len(shards))
        return jnp.repeat(jnp.exp(heights), shape[axis_at] // blocks).reshape((-1,) + (1,) * (len(shape) - axis_at - 1))

    level = one(*shards[0])
    for cut in shards[1:]:
        level = level * one(*cut)
    return level


def normal_values(stream_key, dims, scale, limit, pieces=(), held_as=jnp.bfloat16):
    level = shard_levels(stream_key, dims, pieces, -0.22, 0.18) if pieces else 1.0
    drawn = jax.random.normal(stream_key, dims, jnp.float32) * scale * level
    return jnp.minimum(jnp.maximum(drawn, -limit), limit).astype(held_as)


def setup_inputs(seed: int = 0) -> dict:
    key_of = jax.random.split(jax.random.key(seed), 5)
    signal = normal_values(key_of[0], (LENGTH, CHANNELS), 1.0, 6.0, ((0, 32),))
    filter_param = normal_values(key_of[1], (LENGTH, CHANNELS), 1.0, 6.0, ((0, 32),))
    skip_gain = jnp.clip(jax.random.uniform(key_of[2], (CHANNELS,), jnp.float32, 0.5, 1.5), 0.5, 1.5)
    out_grad = normal_values(key_of[3], (LENGTH, CHANNELS), 1.0, 6.0, ((0, 32),))
    return dict(signal=signal, filter_param=filter_param, skip_gain=skip_gain, out_grad=out_grad)


def reference(signal, filter_param, skip_gain, out_grad):
    scale = 1.0 / math.sqrt(LENGTH)
    filt_spec = jnp.fft.fft(filter_param.astype(jnp.float32), axis=0) * scale
    values = signal.astype(jnp.float32)
    cotan = out_grad.astype(jnp.float32)
    sig_spec = jnp.fft.fft(values, axis=0)
    grad_spec = jnp.fft.fft(cotan, axis=0)
    conv = jnp.real(jnp.fft.ifft(sig_spec * filt_spec, axis=0)) + skip_gain * values
    back = jnp.real(jnp.fft.ifft(jnp.conj(filt_spec) * grad_spec, axis=0)) + skip_gain * cotan
    taps = jnp.real(jnp.fft.ifft(jnp.conj(sig_spec) * grad_spec, axis=0)) * scale
    return (conv.astype(jnp.bfloat16), back.astype(jnp.bfloat16), taps.astype(jnp.float32))
```

```python
import functools
import math

import jax
import jax.numpy as jnp
import ml_dtypes
import numpy as np
from jax import lax
from jax.experimental import pallas as pl
from jax.experimental.pallas import tpu as pltpu
from jax.sharding import PartitionSpec as P

LANES = 128
MESH = pl.DeviceIdType.MESH


def round_up(value, step):
    return -(-value // step) * step


def split_table(table):
    high = table.astype(np.float32).astype(ml_dtypes.bfloat16)
    low = (table - high.astype(np.float64)).astype(np.float32).astype(ml_dtypes.bfloat16)
    return high, low


def make_tables(length, sources):
    outer = length // LANES
    runs = outer // sources
    half = round_up(outer // 2 + 1, 16)
    k1 = np.arange(half)
    a = (np.arange(sources)[None, :] * runs + np.arange(runs)[:, None]).reshape(-1)
    kept = (k1 <= outer // 2).astype(np.float64)
    angle = 2.0 * math.pi * ((k1[:, None] * a[None, :]) % outer) / outer
    left = np.concatenate([np.cos(angle) * kept[:, None], -np.sin(angle) * kept[:, None]], axis=0)
    left = np.concatenate(split_table(left), axis=1)
    b = np.arange(LANES)
    turn = 2.0 * math.pi * ((k1[:, None] * b[None, :]) % length) / length
    twiddle = np.stack([np.cos(turn), -np.sin(turn)]).astype(np.float32)
    inner = 2.0 * math.pi * ((b[:, None] * b[None, :]) % LANES) / LANES
    cos, sin = np.cos(inner), np.sin(inner)
    right = np.stack(split_table(np.block([[cos, -sin], [sin, cos]])))
    right_inv = np.stack(split_table(np.block([[cos, sin], [-sin, cos]])))
    weight = kept * np.where((k1 == 0) | (2 * k1 == outer), 1.0, 2.0) / length
    left_inv = np.concatenate([np.cos(angle) * weight[:, None], -np.sin(angle) * weight[:, None]], axis=0).T
    high, low = split_table(left_inv)
    left_inv = np.concatenate([high, high, low], axis=1)
    return left, twiddle, right, right_inv, left_inv


def split(value):
    high = value.astype(jnp.bfloat16)
    low = (value - high.astype(jnp.float32)).astype(jnp.bfloat16)
    return high, low


def dot(a, b):
    return jnp.dot(a, b, preferred_element_type=jnp.float32)


def right_product(value, table_ref):
    high, low = split(value)
    return dot(high, table_ref[0]) + dot(low, table_ref[0]) + dot(high, table_ref[1])


def kernel(
    devs, inner_devs, scale,
    gain_ref, sig_ref, filt_ref, cot_ref,
    left_hbm, twiddle_hbm, right_hbm, right_inv_hbm, left_inv_hbm,
    conv_ref, back_ref, taps_ref,
    left_ref, twiddle_ref, right_ref, right_inv_ref, left_inv_ref,
    wide_in, send_in, recv_in, wide_out, send_out, recv_out, send_taps, recv_taps,
    table_sem, own_sem, send_sem, recv_sem,
):
    rows, chans = sig_ref.shape
    runs = rows // LANES
    mine = chans // devs
    outer = runs * devs
    half = twiddle_ref.shape[1]
    rows_in = send_in.shape[1]
    rows_out = send_out.shape[1]
    rows_taps = send_taps.shape[1]
    me = lax.axis_index("seq") * inner_devs + lax.axis_index("dp")

    def place(index):
        return (index // inner_devs, lax.rem(index, inner_devs))

    barrier = pltpu.get_barrier_semaphore()

    def greet(step, carry):
        pl.semaphore_signal(barrier, inc=1, device_id=place(lax.rem(me + step, devs)), device_id_type=MESH)
        return carry

    lax.fori_loop(1, devs, greet, 0)

    tables = [
        pltpu.make_async_copy(src, dst, table_sem.at[at])
        for at, (src, dst) in enumerate(
            [
                (left_hbm, left_ref),
                (twiddle_hbm, twiddle_ref),
                (right_hbm, right_ref),
                (right_inv_hbm, right_inv_ref),
                (left_inv_hbm, left_inv_ref),
            ]
        )
    ]
    for copy in tables:
        copy.start()

    for at, ref in enumerate((sig_ref, cot_ref, filt_ref)):
        for run in range(runs):
            block = ref[run * LANES : (run + 1) * LANES, :].astype(jnp.float32).T
            for c in range(mine):
                wide_in[pl.ds((at * mine + c) * runs + run, devs, stride=rows_in), :] = block[
                    c * devs : (c + 1) * devs, :
                ]
    send_in[...] = wide_in[...].astype(jnp.bfloat16).reshape(devs, rows_in, LANES)

    pl.semaphore_wait(barrier, devs - 1)

    def exchange(kind, send, recv):
        own = pltpu.make_async_copy(send.at[me], recv.at[me], own_sem.at[kind])
        own.start()

        def remote(to, slot_from, slot_send):
            return pltpu.make_async_remote_copy(
                src_ref=send.at[to],
                dst_ref=recv.at[slot_from],
                send_sem=send_sem.at[kind, slot_send],
                recv_sem=recv_sem.at[kind, slot_from],
                device_id=place(to),
                device_id_type=MESH,
            )

        def begin(step, carry):
            to = lax.rem(me + step, devs)
            remote(to, me, to).start()
            return carry

        lax.fori_loop(1, devs, begin, 0)

        def finish():
            own.wait()

            def arrive(step, carry):
                other = lax.rem(me + devs - step, devs)
                remote(other, other, other).wait_recv()
                return carry

            lax.fori_loop(1, devs, arrive, 0)

        def drain():
            def left_device(step, carry):
                to = lax.rem(me + step, devs)
                remote(to, me, to).wait_send()
                return carry

            lax.fori_loop(1, devs, left_device, 0)

        return finish, drain

    finish_in, drain_in = exchange(0, send_in, recv_in)
    for copy in tables:
        copy.wait()
    finish_in()
    wide_in[...] = recv_in[...].astype(jnp.float32).reshape(devs * rows_in, LANES)

    def column(at, c):
        return jnp.concatenate(
            [wide_in[pl.ds((at * mine + c) * runs + run, devs, stride=rows_in), :] for run in range(runs)],
            axis=0,
        )

    tw_re, tw_im = twiddle_ref[0], twiddle_ref[1]
    columns = [[column(at, c) for c in range(mine)] for at in range(3)]
    spectra = []
    for at in range(3):
        flat = jnp.concatenate(columns[at], axis=1).astype(jnp.bfloat16)
        partial = dot(left_ref[...], jnp.concatenate([flat, flat], axis=0))
        turned = []
        for c in range(mine):
            re = partial[:half, c * LANES : (c + 1) * LANES]
            im = partial[half:, c * LANES : (c + 1) * LANES]
            turned.append(jnp.concatenate([re * tw_re - im * tw_im, re * tw_im + im * tw_re], axis=1))
        spec = right_product(jnp.concatenate(turned, axis=0), right_ref)
        spectra.append((spec[:, :LANES], spec[:, LANES:]))
    (sig_re, sig_im), (cot_re, cot_im), (filt_re, filt_im) = spectra
    filt_re, filt_im = filt_re * scale, filt_im * scale

    def inverse(re, im):
        unit = right_product(jnp.concatenate([re, im], axis=1), right_inv_ref)
        turned = []
        for c in range(mine):
            u_re = unit[c * half : (c + 1) * half, :LANES]
            u_im = unit[c * half : (c + 1) * half, LANES:]
            turned.append(jnp.concatenate([u_re * tw_re + u_im * tw_im, u_im * tw_re - u_re * tw_im], axis=0))
        high, low = split(jnp.concatenate(turned, axis=1))
        return dot(left_inv_ref[...], jnp.concatenate([high, low, high], axis=0))

    taps = inverse(sig_re * cot_re + sig_im * cot_im, sig_re * cot_im - sig_im * cot_re) * scale
    for c in range(mine):
        for run in range(runs):
            send_taps_rows = taps[run * devs : (run + 1) * devs, c * LANES : (c + 1) * LANES]
            wide_out[pl.ds(c * runs + run, devs, stride=rows_taps), :] = send_taps_rows
    send_taps[...] = wide_out[0 : devs * rows_taps, :].reshape(devs, rows_taps, LANES)
    finish_taps, drain_taps = exchange(1, send_taps, recv_taps)

    gains = [gain_ref[c * devs + me] for c in range(mine)]
    conv = inverse(sig_re * filt_re - sig_im * filt_im, sig_re * filt_im + sig_im * filt_re)
    back = inverse(filt_re * cot_re + filt_im * cot_im, filt_re * cot_im - filt_im * cot_re)
    for at, value in enumerate((conv, back)):
        for c in range(mine):
            done = value[:, c * LANES : (c + 1) * LANES] + gains[c] * columns[at][c]
            for run in range(runs):
                wide_out[pl.ds((at * mine + c) * runs + run, devs, stride=rows_out), :] = done[
                    run * devs : (run + 1) * devs, :
                ]
    send_out[...] = wide_out[0 : devs * rows_out, :].astype(jnp.bfloat16).reshape(devs, rows_out, LANES)
    finish_out, drain_out = exchange(2, send_out, recv_out)

    def place_rows(source, at, stride, out_ref):
        for run in range(runs):
            block = jnp.concatenate(
                [source[pl.ds((at * mine + c) * runs + run, devs, stride=stride), :] for c in range(mine)],
                axis=0,
            )
            out_ref[run * LANES : (run + 1) * LANES, :] = block.T.astype(out_ref.dtype)

    finish_taps()
    wide_in[0 : devs * rows_taps, :] = recv_taps[...].reshape(devs * rows_taps, LANES)
    place_rows(wide_in, 0, rows_taps, taps_ref)
    finish_out()
    wide_in[0 : devs * rows_out, :] = recv_out[...].astype(jnp.float32).reshape(devs * rows_out, LANES)
    place_rows(wide_in, 0, rows_out, conv_ref)
    place_rows(wide_in, 1, rows_out, back_ref)
    drain_in()
    drain_taps()
    drain_out()


def per_device(devs, inner_devs, signal, filter_param, skip_gain, out_grad):
    rows, chans = signal.shape
    length = rows * devs
    mine = chans // devs
    runs = rows // LANES
    rows_in = round_up(3 * mine * runs, 16)
    rows_out = round_up(2 * mine * runs, 16)
    rows_taps = round_up(mine * runs, 8)
    tables = [jnp.asarray(table) for table in make_tables(length, devs)]
    bf16, f32 = jnp.bfloat16, jnp.float32
    vmem = pl.BlockSpec(memory_space=pltpu.VMEM)
    return pl.pallas_call(
        functools.partial(kernel, devs, inner_devs, 1.0 / math.sqrt(length)),
        out_shape=(
            jax.ShapeDtypeStruct((rows, chans), bf16),
            jax.ShapeDtypeStruct((rows, chans), bf16),
            jax.ShapeDtypeStruct((rows, chans), f32),
        ),
        in_specs=[pl.BlockSpec(memory_space=pltpu.SMEM)] + [vmem] * 3 + [pl.BlockSpec(memory_space=pl.ANY)] * 5,
        out_specs=(vmem, vmem, vmem),
        scratch_shapes=[pltpu.VMEM(table.shape, table.dtype) for table in tables]
        + [
            pltpu.VMEM((devs * rows_in, LANES), f32),
            pltpu.VMEM((devs, rows_in, LANES), bf16),
            pltpu.VMEM((devs, rows_in, LANES), bf16),
            pltpu.VMEM((devs * max(rows_out, rows_taps), LANES), f32),
            pltpu.VMEM((devs, rows_out, LANES), bf16),
            pltpu.VMEM((devs, rows_out, LANES), bf16),
            pltpu.VMEM((devs, rows_taps, LANES), f32),
            pltpu.VMEM((devs, rows_taps, LANES), f32),
            pltpu.SemaphoreType.DMA((5,)),
            pltpu.SemaphoreType.DMA((3,)),
            pltpu.SemaphoreType.DMA((3, devs)),
            pltpu.SemaphoreType.DMA((3, devs)),
        ],
        compiler_params=pltpu.CompilerParams(
            collective_id=0, has_side_effects=True, vmem_limit_bytes=48 * 1024 * 1024
        ),
    )(skip_gain, signal, filter_param, out_grad, *tables)


def solution(mesh):
    devs = mesh.shape["seq"] * mesh.shape["dp"]
    rows = P(("seq", "dp"), None)
    return jax.shard_map(
        functools.partial(per_device, devs, mesh.shape["dp"]),
        mesh=mesh,
        in_specs=(rows, rows, P(), rows),
        out_specs=(rows, rows, rows),
        check_vma=False,
    )
```

```python
import functools
import math

import jax
import jax.numpy as jnp
import ml_dtypes
import numpy as np
from jax import lax
from jax.experimental import pallas as pl
from jax.experimental.pallas import tpu as pltpu
from jax.sharding import PartitionSpec as P

LANES = 128
MESH = pl.DeviceIdType.MESH


def round_up(value, step):
    return -(-value // step) * step


def split_table(table):
    high = table.astype(np.float32).astype(ml_dtypes.bfloat16)
    low = (table - high.astype(np.float64)).astype(np.float32).astype(ml_dtypes.bfloat16)
    return high, low


def make_tables(length, sources):
    outer = length // LANES
    runs = outer // sources
    half = round_up(outer // 2 + 1, 16)
    k1 = np.arange(half)
    a = (np.arange(sources)[None, :] * runs + np.arange(runs)[:, None]).reshape(-1)
    kept = (k1 <= outer // 2).astype(np.float64)
    angle = 2.0 * math.pi * ((k1[:, None] * a[None, :]) % outer) / outer
    left = np.concatenate([np.cos(angle) * kept[:, None], -np.sin(angle) * kept[:, None]], axis=0)
    left = np.concatenate(split_table(left), axis=1)
    b = np.arange(LANES)
    turn = 2.0 * math.pi * ((k1[:, None] * b[None, :]) % length) / length
    twiddle = np.stack([np.cos(turn), -np.sin(turn)]).astype(np.float32)
    inner = 2.0 * math.pi * ((b[:, None] * b[None, :]) % LANES) / LANES
    cos, sin = np.cos(inner), np.sin(inner)
    right = np.stack(split_table(np.block([[cos, -sin], [sin, cos]])))
    right_inv = np.stack(split_table(np.block([[cos, sin], [-sin, cos]])))
    weight = kept * np.where((k1 == 0) | (2 * k1 == outer), 1.0, 2.0) / length
    left_inv = np.concatenate([np.cos(angle) * weight[:, None], -np.sin(angle) * weight[:, None]], axis=0).T
    high, low = split_table(left_inv)
    left_inv = np.concatenate([high, high, low], axis=1)
    return left, twiddle, right, right_inv, left_inv


def split(value):
    high = value.astype(jnp.bfloat16)
    low = (value - high.astype(jnp.float32)).astype(jnp.bfloat16)
    return high, low


def dot(a, b):
    return jnp.dot(a, b, preferred_element_type=jnp.float32)


def right_product(value, table_ref):
    high, low = split(value)
    return dot(high, table_ref[0]) + dot(low, table_ref[0]) + dot(high, table_ref[1])


def kernel(
    devs, inner_devs, scale,
    gain_ref, sig_hbm, cot_hbm, filt_hbm,
    left_hbm, twiddle_hbm, right_hbm, right_inv_hbm, left_inv_hbm,
    conv_ref, back_ref, taps_ref,
    sig_ref, cot_ref, filt_ref,
    left_ref, twiddle_ref, right_ref, right_inv_ref, left_inv_ref,
    wide_pair, wide_filt, wide_out,
    send_pair, send_filt, send_taps, send_conv, send_back,
    recv_pair, recv_filt, recv_taps, recv_conv, recv_back,
    load_sem, own_sem, send_sem, recv_sem,
):
    rows, chans = sig_ref.shape
    runs = rows // LANES
    mine = chans // devs
    half = twiddle_ref.shape[1]
    me = lax.axis_index("seq") * inner_devs + lax.axis_index("dp")

    def place(index):
        return (index // inner_devs, lax.rem(index, inner_devs))

    loads = [
        pltpu.make_async_copy(src, dst, load_sem.at[at])
        for at, (src, dst) in enumerate(
            [
                (sig_hbm, sig_ref),
                (cot_hbm, cot_ref),
                (filt_hbm, filt_ref),
                (left_hbm, left_ref),
                (twiddle_hbm, twiddle_ref),
                (right_hbm, right_ref),
                (right_inv_hbm, right_inv_ref),
                (left_inv_hbm, left_inv_ref),
            ]
        )
    ]
    for copy in loads:
        copy.start()

    barrier = pltpu.get_barrier_semaphore()

    def greet(step, carry):
        pl.semaphore_signal(barrier, inc=1, device_id=place(lax.rem(me + step, devs)), device_id_type=MESH)
        return carry

    lax.fori_loop(1, devs, greet, 0)

    def exchange(kind, send, recv):
        own = pltpu.make_async_copy(send.at[me], recv.at[me], own_sem.at[kind])
        own.start()

        def remote(to, slot_from, slot_send):
            return pltpu.make_async_remote_copy(
                src_ref=send.at[to],
                dst_ref=recv.at[slot_from],
                send_sem=send_sem.at[kind, slot_send],
                recv_sem=recv_sem.at[kind, slot_from],
                device_id=place(to),
                device_id_type=MESH,
            )

        def begin(step, carry):
            to = lax.rem(me + step, devs)
            remote(to, me, to).start()
            return carry

        lax.fori_loop(1, devs, begin, 0)

        def finish():
            own.wait()

            def arrive(step, carry):
                other = lax.rem(me + devs - step, devs)
                remote(other, other, other).wait_recv()
                return carry

            lax.fori_loop(1, devs, arrive, 0)

        def drain():
            def leave(step, carry):
                to = lax.rem(me + step, devs)
                remote(to, me, to).wait_send()
                return carry

            lax.fori_loop(1, devs, leave, 0)

        return finish, drain

    def pack(ref, at, wide, stride):
        for run in range(runs):
            block = ref[run * LANES : (run + 1) * LANES, :].astype(jnp.float32).T
            for c in range(mine):
                wide[pl.ds((at * mine + c) * runs + run, devs, stride=stride), :] = block[c * devs : (c + 1) * devs, :]

    def narrow(wide, send):
        send[...] = wide[0 : devs * send.shape[1], :].astype(send.dtype).reshape(send.shape)

    def widen(recv, wide):
        wide[0 : devs * recv.shape[1], :] = recv[...].astype(jnp.float32).reshape(devs * recv.shape[1], LANES)

    rows_pair, rows_filt = send_pair.shape[1], send_filt.shape[1]
    loads[0].wait()
    pack(sig_ref, 0, wide_pair, rows_pair)
    loads[1].wait()
    pack(cot_ref, 1, wide_pair, rows_pair)
    narrow(wide_pair, send_pair)
    pl.semaphore_wait(barrier, devs - 1)
    finish_pair, drain_pair = exchange(0, send_pair, recv_pair)
    loads[2].wait()
    pack(filt_ref, 0, wide_filt, rows_filt)
    narrow(wide_filt, send_filt)
    finish_filt, drain_filt = exchange(1, send_filt, recv_filt)
    for copy in loads[3:]:
        copy.wait()

    tw_re, tw_im = twiddle_ref[0], twiddle_ref[1]

    def columns_of(wide, at, stride):
        return [
            jnp.concatenate(
                [wide[pl.ds((at * mine + c) * runs + run, devs, stride=stride), :] for run in range(runs)], axis=0
            )
            for c in range(mine)
        ]

    def forward(columns):
        flat = jnp.concatenate(columns, axis=1).astype(jnp.bfloat16)
        partial = dot(left_ref[...], jnp.concatenate([flat, flat], axis=0))
        turned = []
        for c in range(mine):
            re = partial[:half, c * LANES : (c + 1) * LANES]
            im = partial[half:, c * LANES : (c + 1) * LANES]
            turned.append(jnp.concatenate([re * tw_re - im * tw_im, re * tw_im + im * tw_re], axis=1))
        spec = right_product(jnp.concatenate(turned, axis=0), right_ref)
        return spec[:, :LANES], spec[:, LANES:]

    def inverse(re, im):
        unit = right_product(jnp.concatenate([re, im], axis=1), right_inv_ref)
        turned = []
        for c in range(mine):
            u_re = unit[c * half : (c + 1) * half, :LANES]
            u_im = unit[c * half : (c + 1) * half, LANES:]
            turned.append(jnp.concatenate([u_re * tw_re + u_im * tw_im, u_im * tw_re - u_re * tw_im], axis=0))
        high, low = split(jnp.concatenate(turned, axis=1))
        return dot(left_inv_ref[...], jnp.concatenate([high, low, high], axis=0))

    def unpack(values, send):
        stride = send.shape[1]
        for c in range(mine):
            for run in range(runs):
                wide_out[pl.ds(c * runs + run, devs, stride=stride), :] = values[c][run * devs : (run + 1) * devs, :]
        narrow(wide_out, send)

    def lanes_of(value):
        return [value[:, c * LANES : (c + 1) * LANES] for c in range(mine)]

    finish_pair()
    widen(recv_pair, wide_pair)
    sig_cols = columns_of(wide_pair, 0, rows_pair)
    cot_cols = columns_of(wide_pair, 1, rows_pair)
    sig_re, sig_im = forward(sig_cols)
    cot_re, cot_im = forward(cot_cols)
    taps = inverse(sig_re * cot_re + sig_im * cot_im, sig_re * cot_im - sig_im * cot_re) * scale
    unpack(lanes_of(taps), send_taps)
    finish_taps, drain_taps = exchange(2, send_taps, recv_taps)

    gains = [gain_ref[c * devs + me] for c in range(mine)]
    finish_filt()
    widen(recv_filt, wide_filt)
    filt_re, filt_im = forward(columns_of(wide_filt, 0, rows_filt))
    filt_re, filt_im = filt_re * scale, filt_im * scale
    conv = lanes_of(inverse(sig_re * filt_re - sig_im * filt_im, sig_re * filt_im + sig_im * filt_re))
    unpack([conv[c] + gains[c] * sig_cols[c] for c in range(mine)], send_conv)
    finish_conv, drain_conv = exchange(3, send_conv, recv_conv)
    back = lanes_of(inverse(filt_re * cot_re + filt_im * cot_im, filt_re * cot_im - filt_im * cot_re))
    unpack([back[c] + gains[c] * cot_cols[c] for c in range(mine)], send_back)
    finish_back, drain_back = exchange(4, send_back, recv_back)

    def deliver(recv, out_ref):
        widen(recv, wide_filt)
        stride = recv.shape[1]
        for run in range(runs):
            block = jnp.concatenate(
                [wide_filt[pl.ds(c * runs + run, devs, stride=stride), :] for c in range(mine)], axis=0
            )
            out_ref[run * LANES : (run + 1) * LANES, :] = block.T.astype(out_ref.dtype)

    drain_pair()
    drain_filt()
    finish_taps()
    deliver(recv_taps, taps_ref)
    finish_conv()
    deliver(recv_conv, conv_ref)
    finish_back()
    deliver(recv_back, back_ref)
    drain_taps()
    drain_conv()
    drain_back()


def per_device(devs, inner_devs, signal, filter_param, skip_gain, out_grad):
    rows, chans = signal.shape
    length = rows * devs
    mine = chans // devs
    runs = rows // LANES
    rows_pair = round_up(2 * mine * runs, 16)
    rows_one = round_up(mine * runs, 16)
    rows_taps = round_up(mine * runs, 8)
    tables = [jnp.asarray(table) for table in make_tables(length, devs)]
    bf16, f32 = jnp.bfloat16, jnp.float32
    vmem = pl.BlockSpec(memory_space=pltpu.VMEM)
    hbm = pl.BlockSpec(memory_space=pltpu.HBM)
    slots = [
        pltpu.VMEM((devs, rows_pair, LANES), bf16),
        pltpu.VMEM((devs, rows_one, LANES), bf16),
        pltpu.VMEM((devs, rows_taps, LANES), f32),
        pltpu.VMEM((devs, rows_one, LANES), bf16),
        pltpu.VMEM((devs, rows_one, LANES), bf16),
    ]
    return pl.pallas_call(
        functools.partial(kernel, devs, inner_devs, 1.0 / math.sqrt(length)),
        out_shape=(
            jax.ShapeDtypeStruct((rows, chans), bf16),
            jax.ShapeDtypeStruct((rows, chans), bf16),
            jax.ShapeDtypeStruct((rows, chans), f32),
        ),
        in_specs=[pl.BlockSpec(memory_space=pltpu.SMEM)] + [hbm] * 8,
        out_specs=(vmem, vmem, vmem),
        scratch_shapes=[pltpu.VMEM((rows, chans), bf16)] * 3
        + [pltpu.VMEM(table.shape, table.dtype) for table in tables]
        + [
            pltpu.VMEM((devs * rows_pair, LANES), f32),
            pltpu.VMEM((devs * rows_one, LANES), f32),
            pltpu.VMEM((devs * rows_one, LANES), f32),
        ]
        + slots
        + slots
        + [
            pltpu.SemaphoreType.DMA((8,)),
            pltpu.SemaphoreType.DMA((5,)),
            pltpu.SemaphoreType.DMA((5, devs)),
            pltpu.SemaphoreType.DMA((5, devs)),
        ],
        compiler_params=pltpu.CompilerParams(
            collective_id=0, has_side_effects=True, vmem_limit_bytes=64 * 1024 * 1024
        ),
    )(skip_gain, signal, out_grad, filter_param, *tables)


def solution(mesh):
    devs = mesh.shape["seq"] * mesh.shape["dp"]
    rows = P(("seq", "dp"), None)
    return jax.shard_map(
        functools.partial(per_device, devs, mesh.shape["dp"]),
        mesh=mesh,
        in_specs=(rows, rows, P(), rows),
        out_specs=(rows, rows, rows),
        check_vma=False,
    )
```

```python
import functools
import math

import jax
import jax.numpy as jnp
import ml_dtypes
import numpy as np
from jax import lax
from jax.experimental import pallas as pl
from jax.experimental.pallas import tpu as pltpu
from jax.sharding import PartitionSpec as P

LANES = 128
MESH = pl.DeviceIdType.MESH


def round_up(value, step):
    return -(-value // step) * step


def split_table(table):
    high = table.astype(np.float32).astype(ml_dtypes.bfloat16)
    low = (table - high.astype(np.float64)).astype(np.float32).astype(ml_dtypes.bfloat16)
    return high, low


def make_tables(length, sources):
    outer = length // LANES
    runs = outer // sources
    half = round_up(outer // 2 + 1, 16)
    k1 = np.arange(half)
    a = (np.arange(sources)[None, :] * runs + np.arange(runs)[:, None]).reshape(-1)
    kept = (k1 <= outer // 2).astype(np.float64)
    angle = 2.0 * math.pi * ((k1[:, None] * a[None, :]) % outer) / outer
    left = np.concatenate([np.cos(angle) * kept[:, None], -np.sin(angle) * kept[:, None]], axis=0)
    left = np.concatenate(split_table(left), axis=1)
    b = np.arange(LANES)
    turn = 2.0 * math.pi * ((k1[:, None] * b[None, :]) % length) / length
    twiddle = np.stack([np.cos(turn), -np.sin(turn)]).astype(np.float32)
    inner = 2.0 * math.pi * ((b[:, None] * b[None, :]) % LANES) / LANES
    cos, sin = np.cos(inner), np.sin(inner)
    right = np.stack(split_table(np.block([[cos, -sin], [sin, cos]])))
    right_inv = np.stack(split_table(np.block([[cos, sin], [-sin, cos]])))
    weight = kept * np.where((k1 == 0) | (2 * k1 == outer), 1.0, 2.0) / length
    left_inv = np.concatenate([np.cos(angle) * weight[:, None], -np.sin(angle) * weight[:, None]], axis=0).T
    high, low = split_table(left_inv)
    left_inv = np.concatenate([high, high, low], axis=1)
    return left, twiddle, right, right_inv, left_inv


def split(value):
    high = value.astype(jnp.bfloat16)
    low = (value - high.astype(jnp.float32)).astype(jnp.bfloat16)
    return high, low


def dot(a, b):
    return jnp.dot(a, b, preferred_element_type=jnp.float32)


def right_product(value, table_ref):
    high, low = split(value)
    return dot(high, table_ref[0]) + dot(low, table_ref[0]) + dot(high, table_ref[1])


def kernel(
    devs, inner_devs, scale,
    gain_ref, sig_hbm, cot_hbm, filt_hbm,
    left_hbm, twiddle_hbm, right_hbm, right_inv_hbm, left_inv_hbm,
    conv_ref, back_ref, taps_ref,
    sig_ref, cot_ref, filt_ref,
    left_ref, twiddle_ref, right_ref, right_inv_ref, left_inv_ref,
    wide_pair, wide_filt, wide_out,
    send_pair, send_filt, send_taps, send_both,
    recv_pair, recv_filt, recv_taps, recv_both,
    load_sem, own_sem, send_sem, recv_sem,
):
    rows, chans = sig_ref.shape
    runs = rows // LANES
    mine = chans // devs
    half = twiddle_ref.shape[1]
    me = lax.axis_index("seq") * inner_devs + lax.axis_index("dp")

    def place(index):
        return (index // inner_devs, lax.rem(index, inner_devs))

    loads = [
        pltpu.make_async_copy(src, dst, load_sem.at[at])
        for at, (src, dst) in enumerate(
            [
                (sig_hbm, sig_ref),
                (cot_hbm, cot_ref),
                (filt_hbm, filt_ref),
                (left_hbm, left_ref),
                (twiddle_hbm, twiddle_ref),
                (right_hbm, right_ref),
                (right_inv_hbm, right_inv_ref),
                (left_inv_hbm, left_inv_ref),
            ]
        )
    ]
    for copy in loads:
        copy.start()

    barrier = pltpu.get_barrier_semaphore()

    def greet(step, carry):
        pl.semaphore_signal(barrier, inc=1, device_id=place(lax.rem(me + step, devs)), device_id_type=MESH)
        return carry

    lax.fori_loop(1, devs, greet, 0)

    def exchange(kind, send, recv):
        own = pltpu.make_async_copy(send.at[me], recv.at[me], own_sem.at[kind])
        own.start()

        def remote(to, src, dst):
            return pltpu.make_async_remote_copy(
                src_ref=src,
                dst_ref=dst,
                send_sem=send_sem.at[kind],
                recv_sem=recv_sem.at[kind],
                device_id=place(to),
                device_id_type=MESH,
            )

        def begin(step, carry):
            to = lax.rem(me + step, devs)
            remote(to, send.at[to], recv.at[me]).start()
            return carry

        lax.fori_loop(1, devs, begin, 0)
        others = pl.ds(0, devs - 1)
        all_of_them = remote(lax.rem(me + 1, devs), send.at[others], recv.at[others])

        def finish():
            own.wait()
            all_of_them.wait_recv()

        return finish, all_of_them.wait_send

    def pack(ref, at, wide, stride):
        for run in range(runs):
            block = ref[run * LANES : (run + 1) * LANES, :].astype(jnp.float32).T
            for c in range(mine):
                wide[pl.ds((at * mine + c) * runs + run, devs, stride=stride), :] = block[c * devs : (c + 1) * devs, :]

    def narrow(wide, send):
        send[...] = wide[0 : devs * send.shape[1], :].astype(send.dtype).reshape(send.shape)

    def widen(recv, wide):
        wide[0 : devs * recv.shape[1], :] = recv[...].astype(jnp.float32).reshape(devs * recv.shape[1], LANES)

    rows_pair, rows_filt = send_pair.shape[1], send_filt.shape[1]
    loads[0].wait()
    pack(sig_ref, 0, wide_pair, rows_pair)
    loads[1].wait()
    pack(cot_ref, 1, wide_pair, rows_pair)
    narrow(wide_pair, send_pair)
    pl.semaphore_wait(barrier, devs - 1)
    finish_pair, drain_pair = exchange(0, send_pair, recv_pair)
    loads[2].wait()
    pack(filt_ref, 0, wide_filt, rows_filt)
    narrow(wide_filt, send_filt)
    finish_filt, drain_filt = exchange(1, send_filt, recv_filt)
    for copy in loads[3:]:
        copy.wait()

    tw_re, tw_im = twiddle_ref[0], twiddle_ref[1]

    def columns_of(wide, at, stride):
        return [
            jnp.concatenate(
                [wide[pl.ds((at * mine + c) * runs + run, devs, stride=stride), :] for run in range(runs)], axis=0
            )
            for c in range(mine)
        ]

    def forward(columns):
        flat = jnp.concatenate(columns, axis=1).astype(jnp.bfloat16)
        partial = dot(left_ref[...], jnp.concatenate([flat, flat], axis=0))
        turned = []
        for c in range(mine):
            re = partial[:half, c * LANES : (c + 1) * LANES]
            im = partial[half:, c * LANES : (c + 1) * LANES]
            turned.append(jnp.concatenate([re * tw_re - im * tw_im, re * tw_im + im * tw_re], axis=1))
        spec = right_product(jnp.concatenate(turned, axis=0), right_ref)
        return spec[:, :LANES], spec[:, LANES:]

    def inverse(re, im):
        unit = right_product(jnp.concatenate([re, im], axis=1), right_inv_ref)
        turned = []
        for c in range(mine):
            u_re = unit[c * half : (c + 1) * half, :LANES]
            u_im = unit[c * half : (c + 1) * half, LANES:]
            turned.append(jnp.concatenate([u_re * tw_re + u_im * tw_im, u_im * tw_re - u_re * tw_im], axis=0))
        high, low = split(jnp.concatenate(turned, axis=1))
        return dot(left_inv_ref[...], jnp.concatenate([high, low, high], axis=0))

    def unpack(values, send, first=0, last=True):
        stride = send.shape[1]
        for c in range(mine):
            for run in range(runs):
                wide_out[pl.ds((first * mine + c) * runs + run, devs, stride=stride), :] = values[c][run * devs : (run + 1) * devs, :]
        if last:
            narrow(wide_out, send)

    def lanes_of(value):
        return [value[:, c * LANES : (c + 1) * LANES] for c in range(mine)]

    finish_pair()
    widen(recv_pair, wide_pair)
    sig_cols = columns_of(wide_pair, 0, rows_pair)
    cot_cols = columns_of(wide_pair, 1, rows_pair)
    sig_re, sig_im = forward(sig_cols)
    cot_re, cot_im = forward(cot_cols)
    taps = inverse(sig_re * cot_re + sig_im * cot_im, sig_re * cot_im - sig_im * cot_re) * scale
    unpack(lanes_of(taps), send_taps)
    finish_taps, drain_taps = exchange(2, send_taps, recv_taps)

    gains = [gain_ref[c * devs + me] for c in range(mine)]
    finish_filt()
    widen(recv_filt, wide_filt)
    filt_re, filt_im = forward(columns_of(wide_filt, 0, rows_filt))
    filt_re, filt_im = filt_re * scale, filt_im * scale
    conv = lanes_of(inverse(sig_re * filt_re - sig_im * filt_im, sig_re * filt_im + sig_im * filt_re))
    unpack([conv[c] + gains[c] * sig_cols[c] for c in range(mine)], send_both, 0, False)
    back = lanes_of(inverse(filt_re * cot_re + filt_im * cot_im, filt_re * cot_im - filt_im * cot_re))
    unpack([back[c] + gains[c] * cot_cols[c] for c in range(mine)], send_both, 1)
    finish_both, drain_both = exchange(3, send_both, recv_both)

    def deliver(recv, out_ref, first=0):
        if first == 0:
            widen(recv, wide_filt)
        stride = recv.shape[1]
        for run in range(runs):
            block = jnp.concatenate(
                [wide_filt[pl.ds((first * mine + c) * runs + run, devs, stride=stride), :] for c in range(mine)], axis=0
            )
            out_ref[run * LANES : (run + 1) * LANES, :] = block.T.astype(out_ref.dtype)

    drain_pair()
    drain_filt()
    finish_taps()
    deliver(recv_taps, taps_ref)
    finish_both()
    deliver(recv_both, conv_ref)
    deliver(recv_both, back_ref, 1)
    drain_taps()
    drain_both()


def per_device(devs, inner_devs, signal, filter_param, skip_gain, out_grad):
    rows, chans = signal.shape
    length = rows * devs
    mine = chans // devs
    runs = rows // LANES
    rows_pair = round_up(2 * mine * runs, 16)
    rows_one = round_up(mine * runs, 16)
    rows_taps = round_up(mine * runs, 8)
    tables = [jnp.asarray(table) for table in make_tables(length, devs)]
    bf16, f32 = jnp.bfloat16, jnp.float32
    vmem = pl.BlockSpec(memory_space=pltpu.VMEM)
    hbm = pl.BlockSpec(memory_space=pltpu.HBM)
    slots = [
        pltpu.VMEM((devs, rows_pair, LANES), bf16),
        pltpu.VMEM((devs, rows_one, LANES), bf16),
        pltpu.VMEM((devs, rows_taps, LANES), f32),
        pltpu.VMEM((devs, rows_pair, LANES), bf16),
    ]
    return pl.pallas_call(
        functools.partial(kernel, devs, inner_devs, 1.0 / math.sqrt(length)),
        out_shape=(
            jax.ShapeDtypeStruct((rows, chans), bf16),
            jax.ShapeDtypeStruct((rows, chans), bf16),
            jax.ShapeDtypeStruct((rows, chans), f32),
        ),
        in_specs=[pl.BlockSpec(memory_space=pltpu.SMEM)] + [hbm] * 8,
        out_specs=(vmem, vmem, vmem),
        scratch_shapes=[pltpu.VMEM((rows, chans), bf16)] * 3
        + [pltpu.VMEM(table.shape, table.dtype) for table in tables]
        + [
            pltpu.VMEM((devs * rows_pair, LANES), f32),
            pltpu.VMEM((devs * rows_pair, LANES), f32),
            pltpu.VMEM((devs * rows_pair, LANES), f32),
        ]
        + slots
        + slots
        + [
            pltpu.SemaphoreType.DMA((8,)),
            pltpu.SemaphoreType.DMA((4,)),
            pltpu.SemaphoreType.DMA((4,)),
            pltpu.SemaphoreType.DMA((4,)),
        ],
        compiler_params=pltpu.CompilerParams(
            collective_id=0, has_side_effects=True, vmem_limit_bytes=64 * 1024 * 1024
        ),
    )(skip_gain, signal, out_grad, filter_param, *tables)


def solution(mesh):
    devs = mesh.shape["seq"] * mesh.shape["dp"]
    rows = P(("seq", "dp"), None)
    return jax.shard_map(
        functools.partial(per_device, devs, mesh.shape["dp"]),
        mesh=mesh,
        in_specs=(rows, rows, P(), rows),
        out_specs=(rows, rows, rows),
        check_vma=False,
    )
```

```python
import functools
import math

import jax
import jax.numpy as jnp
import ml_dtypes
import numpy as np
from jax import lax
from jax.experimental import pallas as pl
from jax.experimental.pallas import tpu as pltpu
from jax.sharding import PartitionSpec as P

LANES = 128
MESH = pl.DeviceIdType.MESH


def round_up(value, step):
    return -(-value // step) * step


def split_table(table):
    high = table.astype(np.float32).astype(ml_dtypes.bfloat16)
    low = (table - high.astype(np.float64)).astype(np.float32).astype(ml_dtypes.bfloat16)
    return high, low


def make_tables(length, sources):
    outer = length // LANES
    runs = outer // sources
    half = round_up(outer // 2 + 1, 16)
    k1 = np.arange(half)
    a = (np.arange(sources)[None, :] * runs + np.arange(runs)[:, None]).reshape(-1)
    kept = (k1 <= outer // 2).astype(np.float64)
    angle = 2.0 * math.pi * ((k1[:, None] * a[None, :]) % outer) / outer
    left = np.concatenate([np.cos(angle) * kept[:, None], -np.sin(angle) * kept[:, None]], axis=0)
    left = np.concatenate(split_table(left), axis=1)
    b = np.arange(LANES)
    turn = 2.0 * math.pi * ((k1[:, None] * b[None, :]) % length) / length
    twiddle = np.stack([np.cos(turn), -np.sin(turn)]).astype(np.float32)
    inner = 2.0 * math.pi * ((b[:, None] * b[None, :]) % LANES) / LANES
    cos, sin = np.cos(inner), np.sin(inner)
    right = np.stack(split_table(np.block([[cos, -sin], [sin, cos]])))
    right_inv = np.stack(split_table(np.block([[cos, sin], [-sin, cos]])))
    weight = kept * np.where((k1 == 0) | (2 * k1 == outer), 1.0, 2.0) / length
    left_inv = np.concatenate([np.cos(angle) * weight[:, None], -np.sin(angle) * weight[:, None]], axis=0).T
    high, low = split_table(left_inv)
    left_inv = np.concatenate([high, high, low], axis=1)
    return left, twiddle, right, right_inv, left_inv


def split(value):
    high = value.astype(jnp.bfloat16)
    low = (value - high.astype(jnp.float32)).astype(jnp.bfloat16)
    return high, low


def dot(a, b):
    return jnp.dot(a, b, preferred_element_type=jnp.float32)


def encode(value, shift):
    value = value * shift
    square = value * value
    return jnp.where(value < 0.0, -square * square, square * square)


def decode(code, shift):
    root = jnp.sqrt(jnp.sqrt(jnp.abs(code))) * (1.0 / shift)
    return jnp.where(code < 0.0, -root, root)


def right_product(value, table_ref):
    high, low = split(value)
    return dot(high, table_ref[0]) + dot(low, table_ref[0]) + dot(high, table_ref[1])


def kernel(
    devs, inner_devs, scale, shift,
    gain_ref, sig_hbm, cot_hbm, filt_hbm,
    left_hbm, twiddle_hbm, right_hbm, right_inv_hbm, left_inv_hbm,
    conv_ref, back_ref, taps_ref,
    sig_ref, cot_ref, filt_ref,
    left_ref, twiddle_ref, right_ref, right_inv_ref, left_inv_ref,
    wide_pair, wide_filt, wide_out,
    send_pair, send_filt, send_taps, send_both,
    recv_pair, recv_filt, recv_taps, recv_both,
    load_sem, own_sem, send_sem, recv_sem,
):
    rows, chans = sig_ref.shape
    runs = rows // LANES
    mine = chans // devs
    half = twiddle_ref.shape[1]
    me = lax.axis_index("seq") * inner_devs + lax.axis_index("dp")

    def place(index):
        return (index // inner_devs, lax.rem(index, inner_devs))

    loads = [
        pltpu.make_async_copy(src, dst, load_sem.at[at])
        for at, (src, dst) in enumerate(
            [
                (sig_hbm, sig_ref),
                (cot_hbm, cot_ref),
                (filt_hbm, filt_ref),
                (left_hbm, left_ref),
                (twiddle_hbm, twiddle_ref),
                (right_hbm, right_ref),
                (right_inv_hbm, right_inv_ref),
                (left_inv_hbm, left_inv_ref),
            ]
        )
    ]
    for copy in loads:
        copy.start()

    barrier = pltpu.get_barrier_semaphore()

    def greet(step, carry):
        pl.semaphore_signal(barrier, inc=1, device_id=place(lax.rem(me + step, devs)), device_id_type=MESH)
        return carry

    lax.fori_loop(1, devs, greet, 0)

    def exchange(kind, send, recv):
        own = pltpu.make_async_copy(send.at[me], recv.at[me], own_sem.at[kind])
        own.start()

        def remote(to, src, dst):
            return pltpu.make_async_remote_copy(
                src_ref=src,
                dst_ref=dst,
                send_sem=send_sem.at[kind],
                recv_sem=recv_sem.at[kind],
                device_id=place(to),
                device_id_type=MESH,
            )

        def begin(step, carry):
            to = lax.rem(me + step, devs)
            remote(to, send.at[to], recv.at[me]).start()
            return carry

        lax.fori_loop(1, devs, begin, 0)
        others = pl.ds(0, devs - 1)
        all_of_them = remote(lax.rem(me + 1, devs), send.at[others], recv.at[others])

        def finish():
            own.wait()
            all_of_them.wait_recv()

        return finish, all_of_them.wait_send

    def pack(ref, at, wide, stride):
        for run in range(runs):
            block = ref[run * LANES : (run + 1) * LANES, :].astype(jnp.float32).T
            for c in range(mine):
                wide[pl.ds((at * mine + c) * runs + run, devs, stride=stride), :] = block[c * devs : (c + 1) * devs, :]

    def narrow(wide, send):
        send[...] = wide[0 : devs * send.shape[1], :].astype(send.dtype).reshape(send.shape)

    def widen(recv, wide):
        wide[0 : devs * recv.shape[1], :] = recv[...].astype(jnp.float32).reshape(devs * recv.shape[1], LANES)

    rows_pair, rows_filt = send_pair.shape[1], send_filt.shape[1]
    loads[0].wait()
    pack(sig_ref, 0, wide_pair, rows_pair)
    loads[1].wait()
    pack(cot_ref, 1, wide_pair, rows_pair)
    narrow(wide_pair, send_pair)
    pl.semaphore_wait(barrier, devs - 1)
    finish_pair, drain_pair = exchange(0, send_pair, recv_pair)
    loads[2].wait()
    pack(filt_ref, 0, wide_filt, rows_filt)
    narrow(wide_filt, send_filt)
    finish_filt, drain_filt = exchange(1, send_filt, recv_filt)
    for copy in loads[3:]:
        copy.wait()

    tw_re, tw_im = twiddle_ref[0], twiddle_ref[1]

    def columns_of(wide, at, stride):
        return [
            jnp.concatenate(
                [wide[pl.ds((at * mine + c) * runs + run, devs, stride=stride), :] for run in range(runs)], axis=0
            )
            for c in range(mine)
        ]

    def forward(columns):
        flat = jnp.concatenate(columns, axis=1).astype(jnp.bfloat16)
        partial = dot(left_ref[...], jnp.concatenate([flat, flat], axis=0))
        turned = []
        for c in range(mine):
            re = partial[:half, c * LANES : (c + 1) * LANES]
            im = partial[half:, c * LANES : (c + 1) * LANES]
            turned.append(jnp.concatenate([re * tw_re - im * tw_im, re * tw_im + im * tw_re], axis=1))
        spec = right_product(jnp.concatenate(turned, axis=0), right_ref)
        return spec[:, :LANES], spec[:, LANES:]

    def inverse(re, im):
        unit = right_product(jnp.concatenate([re, im], axis=1), right_inv_ref)
        turned = []
        for c in range(mine):
            u_re = unit[c * half : (c + 1) * half, :LANES]
            u_im = unit[c * half : (c + 1) * half, LANES:]
            turned.append(jnp.concatenate([u_re * tw_re + u_im * tw_im, u_im * tw_re - u_re * tw_im], axis=0))
        high, low = split(jnp.concatenate(turned, axis=1))
        return dot(left_inv_ref[...], jnp.concatenate([high, low, high], axis=0))

    def unpack(values, send, first=0, last=True):
        stride = send.shape[1]
        for c in range(mine):
            for run in range(runs):
                wide_out[pl.ds((first * mine + c) * runs + run, devs, stride=stride), :] = values[c][run * devs : (run + 1) * devs, :]
        if last:
            narrow(wide_out, send)

    def lanes_of(value):
        return [value[:, c * LANES : (c + 1) * LANES] for c in range(mine)]

    finish_pair()
    widen(recv_pair, wide_pair)
    sig_cols = columns_of(wide_pair, 0, rows_pair)
    cot_cols = columns_of(wide_pair, 1, rows_pair)
    sig_re, sig_im = forward(sig_cols)
    cot_re, cot_im = forward(cot_cols)
    taps = inverse(sig_re * cot_re + sig_im * cot_im, sig_re * cot_im - sig_im * cot_re) * scale
    unpack(lanes_of(encode(taps, shift)), send_taps)
    finish_taps, drain_taps = exchange(2, send_taps, recv_taps)

    gains = [gain_ref[c * devs + me] for c in range(mine)]
    finish_filt()
    widen(recv_filt, wide_filt)
    filt_re, filt_im = forward(columns_of(wide_filt, 0, rows_filt))
    filt_re, filt_im = filt_re * scale, filt_im * scale
    conv = lanes_of(inverse(sig_re * filt_re - sig_im * filt_im, sig_re * filt_im + sig_im * filt_re))
    unpack([conv[c] + gains[c] * sig_cols[c] for c in range(mine)], send_both, 0, False)
    back = lanes_of(inverse(filt_re * cot_re + filt_im * cot_im, filt_re * cot_im - filt_im * cot_re))
    unpack([back[c] + gains[c] * cot_cols[c] for c in range(mine)], send_both, 1)
    finish_both, drain_both = exchange(3, send_both, recv_both)

    def deliver(recv, out_ref, first=0, shift=None):
        if first == 0:
            widen(recv, wide_filt)
        stride = recv.shape[1]
        for run in range(runs):
            block = jnp.concatenate(
                [wide_filt[pl.ds((first * mine + c) * runs + run, devs, stride=stride), :] for c in range(mine)], axis=0
            )
            block = block if shift is None else decode(block, shift)
            out_ref[run * LANES : (run + 1) * LANES, :] = block.T.astype(out_ref.dtype)

    drain_pair()
    drain_filt()
    finish_taps()
    deliver(recv_taps, taps_ref, shift=shift)
    finish_both()
    deliver(recv_both, conv_ref)
    deliver(recv_both, back_ref, 1)
    drain_taps()
    drain_both()


def hand_over(conv_ref, back_ref, taps_ref, conv_out, back_out, taps_out, sem):
    copies = [
        pltpu.make_async_copy(src, dst, sem.at[at])
        for at, (src, dst) in enumerate(((conv_ref, conv_out), (back_ref, back_out), (taps_ref, taps_out)))
    ]
    for copy in copies:
        copy.start()
    for copy in copies:
        copy.wait()


def per_device(devs, inner_devs, signal, filter_param, skip_gain, out_grad):
    rows, chans = signal.shape
    length = rows * devs
    mine = chans // devs
    runs = rows // LANES
    rows_pair = round_up(2 * mine * runs, 16)
    rows_one = round_up(mine * runs, 16)
    shift = 2.0 ** (31 - math.ceil(math.log2(36.0 * math.sqrt(length))))
    tables = [jnp.asarray(table) for table in make_tables(length, devs)]
    bf16, f32 = jnp.bfloat16, jnp.float32
    vmem = pl.BlockSpec(memory_space=pltpu.VMEM)
    hbm = pl.BlockSpec(memory_space=pltpu.HBM)
    slots = [
        pltpu.VMEM((devs, rows_pair, LANES), bf16),
        pltpu.VMEM((devs, rows_one, LANES), bf16),
        pltpu.VMEM((devs, rows_one, LANES), bf16),
        pltpu.VMEM((devs, rows_pair, LANES), bf16),
    ]
    shapes = (
        jax.ShapeDtypeStruct((rows, chans), bf16),
        jax.ShapeDtypeStruct((rows, chans), bf16),
        jax.ShapeDtypeStruct((rows, chans), f32),
    )
    made = pl.pallas_call(
        functools.partial(kernel, devs, inner_devs, 1.0 / math.sqrt(length), shift),
        out_shape=shapes,
        in_specs=[pl.BlockSpec(memory_space=pltpu.SMEM)] + [hbm] * 8,
        out_specs=(vmem, vmem, vmem),
        scratch_shapes=[pltpu.VMEM((rows, chans), bf16)] * 3
        + [pltpu.VMEM(table.shape, table.dtype) for table in tables]
        + [
            pltpu.VMEM((devs * rows_pair, LANES), f32),
            pltpu.VMEM((devs * rows_pair, LANES), f32),
            pltpu.VMEM((devs * rows_pair, LANES), f32),
        ]
        + slots
        + slots
        + [
            pltpu.SemaphoreType.DMA((8,)),
            pltpu.SemaphoreType.DMA((4,)),
            pltpu.SemaphoreType.DMA((4,)),
            pltpu.SemaphoreType.DMA((4,)),
        ],
        compiler_params=pltpu.CompilerParams(
            collective_id=0, has_side_effects=True, vmem_limit_bytes=64 * 1024 * 1024
        ),
    )(skip_gain, signal, out_grad, filter_param, *tables)
    place = pl.BlockSpec(memory_space=pl.ANY)
    return pl.pallas_call(
        hand_over,
        out_shape=shapes,
        in_specs=[vmem] * 3,
        out_specs=[place] * 3,
        scratch_shapes=[pltpu.SemaphoreType.DMA((3,))],
    )(*made)


def solution(mesh):
    devs = mesh.shape["seq"] * mesh.shape["dp"]
    rows = P(("seq", "dp"), None)
    return jax.shard_map(
        functools.partial(per_device, devs, mesh.shape["dp"]),
        mesh=mesh,
        in_specs=(rows, rows, P(), rows),
        out_specs=(rows, rows, rows),
        check_vma=False,
    )
```

```python
import functools
import math

import jax
import jax.numpy as jnp
import ml_dtypes
import numpy as np
from jax import lax
from jax.experimental import pallas as pl
from jax.experimental.pallas import tpu as pltpu
from jax.sharding import PartitionSpec as P

LANES = 128
MESH = pl.DeviceIdType.MESH


def round_up(value, step):
    return -(-value // step) * step


def split_table(table):
    high = table.astype(np.float32).astype(ml_dtypes.bfloat16)
    low = (table - high.astype(np.float64)).astype(np.float32).astype(ml_dtypes.bfloat16)
    return high, low


def make_tables(length, sources):
    outer = length // LANES
    runs = outer // sources
    half = round_up(outer // 2 + 1, 16)
    k1 = np.arange(half)
    a = (np.arange(sources)[None, :] * runs + np.arange(runs)[:, None]).reshape(-1)
    kept = (k1 <= outer // 2).astype(np.float64)
    angle = 2.0 * math.pi * ((k1[:, None] * a[None, :]) % outer) / outer
    left = np.concatenate([np.cos(angle) * kept[:, None], -np.sin(angle) * kept[:, None]], axis=0)
    left = np.concatenate(split_table(left), axis=1)
    b = np.arange(LANES)
    turn = 2.0 * math.pi * ((k1[:, None] * b[None, :]) % length) / length
    twiddle = np.stack([np.cos(turn), -np.sin(turn)]).astype(np.float32)
    inner = 2.0 * math.pi * ((b[:, None] * b[None, :]) % LANES) / LANES
    cos, sin = np.cos(inner), np.sin(inner)
    right = np.stack(split_table(np.block([[cos, -sin], [sin, cos]])))
    right_inv = np.stack(split_table(np.block([[cos, sin], [-sin, cos]])))
    weight = kept * np.where((k1 == 0) | (2 * k1 == outer), 1.0, 2.0) / length
    left_inv = np.concatenate([np.cos(angle) * weight[:, None], -np.sin(angle) * weight[:, None]], axis=0).T
    high, low = split_table(left_inv)
    left_inv = np.concatenate([high, high, low], axis=1)
    return left, twiddle, right, right_inv, left_inv


def split(value):
    high = value.astype(jnp.bfloat16)
    low = (value - high.astype(jnp.float32)).astype(jnp.bfloat16)
    return high, low


def dot(a, b):
    return jnp.dot(a, b, preferred_element_type=jnp.float32)


def encode(value, shift):
    value = value * shift
    square = value * value
    return jnp.where(value < 0.0, -square * square, square * square)


def decode(code, shift):
    root = jnp.sqrt(jnp.sqrt(jnp.abs(code))) * (1.0 / shift)
    return jnp.where(code < 0.0, -root, root)


def right_product(value, table_ref):
    high, low = split(value)
    return dot(high, table_ref[0]) + dot(low, table_ref[0]) + dot(high, table_ref[1])


def kernel(
    devs, inner_devs, scale, shift,
    gain_hbm, sig_hbm, cot_hbm, filt_hbm,
    left_hbm, twiddle_hbm, right_hbm, right_inv_hbm, left_inv_hbm,
    conv_hbm, back_hbm, taps_hbm,
    conv_ref, back_ref, taps_ref,
    sig_ref, cot_ref, filt_ref,
    left_ref, twiddle_ref, right_ref, right_inv_ref, left_inv_ref,
    wide_pair, wide_filt, wide_out,
    send_pair, send_filt, send_taps, send_both,
    recv_pair, recv_filt, recv_taps, recv_both,
    gain_ref, load_sem, own_sem, send_sem, recv_sem, store_sem,
):
    rows, chans = sig_ref.shape
    runs = rows // LANES
    mine = chans // devs
    half = twiddle_ref.shape[1]
    me = lax.axis_index("seq") * inner_devs + lax.axis_index("dp")

    def place(index):
        return (index // inner_devs, lax.rem(index, inner_devs))

    loads = [
        pltpu.make_async_copy(src, dst, load_sem.at[at])
        for at, (src, dst) in enumerate(
            [
                (sig_hbm, sig_ref),
                (cot_hbm, cot_ref),
                (filt_hbm, filt_ref),
                (left_hbm, left_ref),
                (twiddle_hbm, twiddle_ref),
                (right_hbm, right_ref),
                (right_inv_hbm, right_inv_ref),
                (left_inv_hbm, left_inv_ref),
                (gain_hbm, gain_ref),
            ]
        )
    ]
    for copy in loads:
        copy.start()

    barrier = pltpu.get_barrier_semaphore()

    def greet(step, carry):
        pl.semaphore_signal(barrier, inc=1, device_id=place(lax.rem(me + step, devs)), device_id_type=MESH)
        return carry

    lax.fori_loop(1, devs, greet, 0)

    def exchange(kind, send, recv):
        own = pltpu.make_async_copy(send.at[me], recv.at[me], own_sem.at[kind])
        own.start()

        def remote(to, src, dst):
            return pltpu.make_async_remote_copy(
                src_ref=src,
                dst_ref=dst,
                send_sem=send_sem.at[kind],
                recv_sem=recv_sem.at[kind],
                device_id=place(to),
                device_id_type=MESH,
            )

        def begin(step, carry):
            to = lax.rem(me + step, devs)
            remote(to, send.at[to], recv.at[me]).start()
            return carry

        lax.fori_loop(1, devs, begin, 0)
        others = pl.ds(0, devs - 1)
        all_of_them = remote(lax.rem(me + 1, devs), send.at[others], recv.at[others])

        def finish():
            own.wait()
            all_of_them.wait_recv()

        return finish, all_of_them.wait_send

    def pack(ref, at, wide, stride):
        for run in range(runs):
            block = ref[run * LANES : (run + 1) * LANES, :].astype(jnp.float32).T
            for c in range(mine):
                wide[pl.ds((at * mine + c) * runs + run, devs, stride=stride), :] = block[c * devs : (c + 1) * devs, :]

    def narrow(wide, send):
        send[...] = wide[0 : devs * send.shape[1], :].astype(send.dtype).reshape(send.shape)

    def widen(recv, wide):
        wide[0 : devs * recv.shape[1], :] = recv[...].astype(jnp.float32).reshape(devs * recv.shape[1], LANES)

    rows_pair, rows_filt = send_pair.shape[1], send_filt.shape[1]
    loads[0].wait()
    pack(sig_ref, 0, wide_pair, rows_pair)
    loads[1].wait()
    pack(cot_ref, 1, wide_pair, rows_pair)
    narrow(wide_pair, send_pair)
    pl.semaphore_wait(barrier, devs - 1)
    finish_pair, drain_pair = exchange(0, send_pair, recv_pair)
    loads[2].wait()
    pack(filt_ref, 0, wide_filt, rows_filt)
    narrow(wide_filt, send_filt)
    finish_filt, drain_filt = exchange(1, send_filt, recv_filt)
    for copy in loads[3:]:
        copy.wait()

    tw_re, tw_im = twiddle_ref[0], twiddle_ref[1]

    def columns_of(wide, at, stride):
        return [
            jnp.concatenate(
                [wide[pl.ds((at * mine + c) * runs + run, devs, stride=stride), :] for run in range(runs)], axis=0
            )
            for c in range(mine)
        ]

    def forward(columns):
        flat = jnp.concatenate(columns, axis=1).astype(jnp.bfloat16)
        partial = dot(left_ref[...], jnp.concatenate([flat, flat], axis=0))
        turned = []
        for c in range(mine):
            re = partial[:half, c * LANES : (c + 1) * LANES]
            im = partial[half:, c * LANES : (c + 1) * LANES]
            turned.append(jnp.concatenate([re * tw_re - im * tw_im, re * tw_im + im * tw_re], axis=1))
        spec = right_product(jnp.concatenate(turned, axis=0), right_ref)
        return spec[:, :LANES], spec[:, LANES:]

    def inverse(re, im):
        unit = right_product(jnp.concatenate([re, im], axis=1), right_inv_ref)
        turned = []
        for c in range(mine):
            u_re = unit[c * half : (c + 1) * half, :LANES]
            u_im = unit[c * half : (c + 1) * half, LANES:]
            turned.append(jnp.concatenate([u_re * tw_re + u_im * tw_im, u_im * tw_re - u_re * tw_im], axis=0))
        high, low = split(jnp.concatenate(turned, axis=1))
        return dot(left_inv_ref[...], jnp.concatenate([high, low, high], axis=0))

    def unpack(values, send, first=0, last=True):
        stride = send.shape[1]
        for c in range(mine):
            for run in range(runs):
                wide_out[pl.ds((first * mine + c) * runs + run, devs, stride=stride), :] = values[c][run * devs : (run + 1) * devs, :]
        if last:
            narrow(wide_out, send)

    def lanes_of(value):
        return [value[:, c * LANES : (c + 1) * LANES] for c in range(mine)]

    finish_pair()
    widen(recv_pair, wide_pair)
    sig_cols = columns_of(wide_pair, 0, rows_pair)
    cot_cols = columns_of(wide_pair, 1, rows_pair)
    sig_re, sig_im = forward(sig_cols)
    cot_re, cot_im = forward(cot_cols)
    taps = inverse(sig_re * cot_re + sig_im * cot_im, sig_re * cot_im - sig_im * cot_re) * scale
    unpack(lanes_of(encode(taps, shift)), send_taps)
    finish_taps, drain_taps = exchange(2, send_taps, recv_taps)

    gains = [gain_ref[c * devs + me] for c in range(mine)]
    finish_filt()
    widen(recv_filt, wide_filt)
    filt_re, filt_im = forward(columns_of(wide_filt, 0, rows_filt))
    filt_re, filt_im = filt_re * scale, filt_im * scale
    conv = lanes_of(inverse(sig_re * filt_re - sig_im * filt_im, sig_re * filt_im + sig_im * filt_re))
    unpack([conv[c] + gains[c] * sig_cols[c] for c in range(mine)], send_both, 0, False)
    back = lanes_of(inverse(filt_re * cot_re + filt_im * cot_im, filt_re * cot_im - filt_im * cot_re))
    unpack([back[c] + gains[c] * cot_cols[c] for c in range(mine)], send_both, 1)
    finish_both, drain_both = exchange(3, send_both, recv_both)

    def deliver(recv, out_ref, first=0, shift=None):
        if first == 0:
            widen(recv, wide_filt)
        stride = recv.shape[1]
        for run in range(runs):
            block = jnp.concatenate(
                [wide_filt[pl.ds((first * mine + c) * runs + run, devs, stride=stride), :] for c in range(mine)], axis=0
            )
            block = block if shift is None else decode(block, shift)
            out_ref[run * LANES : (run + 1) * LANES, :] = block.T.astype(out_ref.dtype)

    stores = [
        pltpu.make_async_copy(src, dst, store_sem.at[at])
        for at, (src, dst) in enumerate(((taps_ref, taps_hbm), (conv_ref, conv_hbm), (back_ref, back_hbm)))
    ]
    drain_pair()
    drain_filt()
    finish_taps()
    deliver(recv_taps, taps_ref, shift=shift)
    stores[0].start()
    finish_both()
    deliver(recv_both, conv_ref)
    stores[1].start()
    deliver(recv_both, back_ref, 1)
    stores[2].start()
    drain_taps()
    drain_both()
    for copy in stores:
        copy.wait()


def hand_over(conv_ref, back_ref, taps_ref, conv_out, back_out, taps_out, sem):
    copies = [
        pltpu.make_async_copy(src, dst, sem.at[at])
        for at, (src, dst) in enumerate(((conv_ref, conv_out), (back_ref, back_out), (taps_ref, taps_out)))
    ]
    for copy in copies:
        copy.start()
    for copy in copies:
        copy.wait()


def per_device(devs, inner_devs, signal, filter_param, skip_gain, out_grad):
    rows, chans = signal.shape
    length = rows * devs
    mine = chans // devs
    runs = rows // LANES
    rows_pair = round_up(2 * mine * runs, 16)
    rows_one = round_up(mine * runs, 16)
    shift = 2.0 ** (31 - math.ceil(math.log2(36.0 * math.sqrt(length))))
    tables = [jnp.asarray(table) for table in make_tables(length, devs)]
    bf16, f32 = jnp.bfloat16, jnp.float32
    vmem = pl.BlockSpec(memory_space=pltpu.VMEM)
    hbm = pl.BlockSpec(memory_space=pltpu.HBM)
    slots = [
        pltpu.VMEM((devs, rows_pair, LANES), bf16),
        pltpu.VMEM((devs, rows_one, LANES), bf16),
        pltpu.VMEM((devs, rows_one, LANES), bf16),
        pltpu.VMEM((devs, rows_pair, LANES), bf16),
    ]
    shapes = (
        jax.ShapeDtypeStruct((rows, chans), bf16),
        jax.ShapeDtypeStruct((rows, chans), bf16),
        jax.ShapeDtypeStruct((rows, chans), f32),
    )
    made = pl.pallas_call(
        functools.partial(kernel, devs, inner_devs, 1.0 / math.sqrt(length), shift),
        out_shape=shapes,
        in_specs=[hbm] * 9,
        out_specs=(hbm, hbm, hbm),
        scratch_shapes=[pltpu.VMEM(shape.shape, shape.dtype) for shape in shapes]
        + [pltpu.VMEM((rows, chans), bf16)] * 3
        + [pltpu.VMEM(table.shape, table.dtype) for table in tables]
        + [
            pltpu.VMEM((devs * rows_pair, LANES), f32),
            pltpu.VMEM((devs * rows_pair, LANES), f32),
            pltpu.VMEM((devs * rows_pair, LANES), f32),
        ]
        + slots
        + slots
        + [
            pltpu.SMEM((chans,), f32),
            pltpu.SemaphoreType.DMA((9,)),
            pltpu.SemaphoreType.DMA((4,)),
            pltpu.SemaphoreType.DMA((4,)),
            pltpu.SemaphoreType.DMA((4,)),
            pltpu.SemaphoreType.DMA((3,)),
        ],
        compiler_params=pltpu.CompilerParams(
            collective_id=0, has_side_effects=True, vmem_limit_bytes=64 * 1024 * 1024
        ),
    )(skip_gain, signal, out_grad, filter_param, *tables)
    place = pl.BlockSpec(memory_space=pl.ANY)
    return pl.pallas_call(
        hand_over,
        out_shape=shapes,
        in_specs=[vmem] * 3,
        out_specs=[place] * 3,
        scratch_shapes=[pltpu.SemaphoreType.DMA((3,))],
    )(*made)


def solution(mesh):
    devs = mesh.shape["seq"] * mesh.shape["dp"]
    rows = P(("seq", "dp"), None)
    return jax.shard_map(
        functools.partial(per_device, devs, mesh.shape["dp"]),
        mesh=mesh,
        in_specs=(rows, rows, P(), rows),
        out_specs=(rows, rows, rows),
        check_vma=False,
    )
```
